32 devices in a mesh: pop: 2 (over y), exp: 16 (over z, x, core), tp: 1.
Axes of the slice: x: 2, y: 2, z: 4, core: 2. Of those that a mesh axis runs over, the one named last changes fastest.
Arguments:
- tokens: bfloat16 [2048, 2880], P(('pop', 'exp'), 'tp'), parts along dimension 0, may hold values from -6 to 6
- routes: int32 [2048, 4], P(('pop', 'exp')), parts along dimension 0, may hold values from 0 to 7, all different within a row; in each aligned block of 64 rows (0 to 63, 64 to 127, ...) at most 64 rows name the same one
- router_weight: bfloat16 [2880, 8], P('tp'), may hold values from -0.109375 to 0.109375
- router_bias: float32 [8], replicated, may hold values from -120 to 163
- member_seeds: int32 [4], P('pop'), parts along dimension 0, may hold values from 0 to 16777215
- gate_weight: bfloat16 [16, 2880, 768], P('exp', None, 'tp'), may hold values from -0.109375 to 0.109375
- up_weight: bfloat16 [16, 2880, 768], P('exp', None, 'tp'), may hold values from -0.109375 to 0.109375
Outputs:
- routed_activations: bfloat16 [2048, 4, 2, 768], P(('pop', 'exp'), None, None, 'tp'), parts along dimension 0
The draws below stay inside these ranges and needn't reach their ends.
There are 2 independent parts, one for each index of `pop`. The reference program is written for one: setup_inputs(seed, part) draws one part's arguments, and reference() takes and returns one part's arrays. A program takes and returns all parts, laid end to end along the dimension named above; an argument that names none is the same for every part. Nothing has to cross between parts.
Inputs may be any that keep to these rules, and one draw needn't show every extreme that they name: `routes`: no expert is named by more than 64 of the 64 rows of one device, and in some device's rows one expert is named exactly 64 times.
All inputs are finite; a program needn't handle non-finite values.
Results may differ from the reference program's by a relative error of at most 0.0049.
Values may be sent and summed in bfloat16 or wider, within the bound.
A program may use at most 64 MiB of HBM per device.

```python
import math
import jax
import jax.numpy as jnp
import numpy as np
from jax import lax

D = 2880
FW = 1536
TOP = 4
LENGTH = 512
TOK_DEV = 64
EXPERTS = 8
CAP_SEND = 64
TOKENS = 1024
TRANSCRIPTS = 2
N_EXP = 16


def draw_router_bias(key, part):
    key = jax.random.fold_in(key, 7)
    return jax.random.normal(key, (EXPERTS,), jnp.float32)


def steps_of(stream_key, shape, cuts, least, top_value):
    factor_of = 1.0
    for position, parts in cuts:
        heights = jax.random.uniform(jax.random.fold_in(jax.random.fold_in(stream_key, 6), position), (parts,), jnp.float32, least / len(cuts), top_value / len(cuts))
        factor_of = factor_of * jnp.repeat(jnp.exp(heights), shape[position] // parts).reshape((-1,) + (1,) * (len(shape) - 1 - position))
    return factor_of


def routed_block(stream_key, own, number, rows, count, top, reach, skew):
    order = jax.random.permutation(stream_key, count)
    heavy_load, ordinary = load_shares(count, rows * top, reach, skew, True), load_shares(count, rows * top, reach, skew, False)
    places = jnp.arange(count)

    def named(sizes, rotation):
        used = int((sizes > 0).sum())
        fixed = max(1, used // 4)
        moved = fixed + (places - fixed + rotation * (used - fixed)) % max(1, count - fixed)
        return jnp.zeros((count,), jnp.int32).at[order[jnp.where(places < fixed, places, moved)]].set(jnp.asarray(sizes, jnp.int32))

    sizes = jnp.where(number % 4 == 0, named(heavy_load, number // 4), named(ordinary, number - number // 4 - 1))
    mixed = jax.random.permutation(jax.random.fold_in(own, 3), count)
    giver, receiver = mixed[0:count // 2 * 2:2], mixed[1:count // 2 * 2:2]
    room = jnp.minimum(sizes[giver] - 1, reach - sizes[receiver]) // 2
    room = jnp.where((giver == order[0]) | (receiver == order[0]) | (sizes[receiver] == 0), 0, jnp.maximum(room, 0))
    moved = jax.random.randint(jax.random.fold_in(own, 4), (count // 2,), 0, 1 << 20) % (room + 1)
    sizes = sizes.at[giver].add(-moved).at[receiver].add(moved)
    items = jnp.searchsorted(jnp.cumsum(sizes), jnp.arange(rows * top), side="right").astype(jnp.int32)
    grid = items.reshape(top, rows).T
    grid = grid[jax.random.permutation(jax.random.fold_in(own, 1), rows)]
    rotation = jax.random.randint(jax.random.fold_in(own, 2), (rows, 1), 0, top)
    return jnp.take_along_axis(grid, (jnp.arange(top)[None, :] + rotation) % top, axis=1)


def load_shares(count, total, most, slope, full):
    weights = [(1 << 20) // math.isqrt(grade ** slope) + 1 for grade in range(1, count + 1)]
    largest = most if full else min(most, max(-(-total // count), total * weights[0] // sum(weights)))
    least = 1 if total - largest >= count - 1 else 0
    given, rest = [largest] + [least] * (count - 1), total - largest - least * (count - 1)
    while rest > 0:
        free = [i for i in range(1, count) if given[i] < largest] or [i for i in range(1, count) if given[i] < most]
        pool, remaining = sum([weights[i] for i in free]), rest
        for i in free:
            extra = min(most - given[i], max(1, remaining * weights[i] // pool), rest)
            given[i] = given[i] + extra
            rest = rest - extra
    return np.array(given)


def normal_values(own_key, shape, spread, limit, cuts=(), held_as=jnp.bfloat16):
    values = jax.random.normal(own_key, shape, jnp.float32) * spread
    if len(cuts) > 0:
        values = steps_of(own_key, shape, cuts, -0.22, 0.18) * values
    return jnp.clip(values, min=-limit, max=limit).astype(held_as)


def setup_inputs(seed: int = 0, part: int = 0) -> dict:
    seeds = jax.random.split(jax.random.key(seed), 8)
    part_keys = jax.random.split(jax.random.fold_in(seeds[7], part), 8)
    tokens = normal_values(part_keys[0], (TOKENS, D), 1.0, 6.0, ((0, 16),))
    routes_keys = jax.random.split(jax.random.fold_in(part_keys[1], 1), TOKENS // TOK_DEV)
    routes_turns = jax.random.permutation(jax.random.fold_in(part_keys[1], 3), TOKENS // TOK_DEV)
    routes = jax.vmap(lambda own, number: routed_block(jax.random.fold_in(part_keys[1], 2), own, number, TOK_DEV, EXPERTS, TOP, CAP_SEND, 2))(routes_keys, routes_turns).reshape((TOKENS, TOP))
    router_weight = normal_values(seeds[2], (D, EXPERTS), D ** -0.5, 0.109375)
    router_bias = draw_router_bias(jax.random.fold_in(seeds[7], 71), part)
    member_seeds = jax.random.randint(part_keys[4], (TRANSCRIPTS,), 0, 16777216).astype(jnp.int32)
    gate_weight = normal_values(seeds[5], (2 * EXPERTS, D, FW // 2), D ** -0.5, 0.109375, ((0, 16),))
    up_weight = normal_values(seeds[6], (2 * EXPERTS, D, FW // 2), D ** -0.5, 0.109375, ((0, 16),))
    return {"tokens": tokens, "routes": routes, "router_weight": router_weight, "router_bias": router_bias, "member_seeds": member_seeds, "gate_weight": gate_weight, "up_weight": up_weight}


NOISE = 0.25
ALPHA = 1.702

def noise_table(member_seeds, matrix_tag, expert, positions, expert_count):
    rank_index = jnp.arange(4, dtype=jnp.int32)
    counter = ((matrix_tag * expert_count + expert) * 4 + rank_index) * 4096
    counter = counter[None, None, :] + positions.astype(jnp.int32)[:, None, None]
    hashed = (member_seeds.astype(jnp.int32)[None, :, None] * 31 + counter) * 1103515245 + 12345
    hashed = hashed ^ hashed >> 16
    hashed = hashed * 747796405
    levels = (hashed >> 16 & 255) - 128
    return (levels.astype(jnp.float32) / 128.0).reshape(positions.shape[0], -1)

def expert_rows(inputs, transcripts, member_seeds, gate_cols, up_cols, expert, hidden_index, expert_count):
    model_width = inputs.shape[1]
    members = member_seeds.shape[0]
    positions = jnp.arange(model_width, dtype=jnp.int32)
    left_factors = jnp.concatenate([noise_table(member_seeds, 0, expert, positions, expert_count), noise_table(member_seeds, 1, expert, positions, expert_count)], axis=1).astype(jnp.bfloat16)
    projected = jnp.dot(inputs, left_factors, preferred_element_type=jnp.float32)
    select = (transcripts[:, None] == jnp.arange(members, dtype=jnp.int32)[None, :]).astype(jnp.float32)
    select = jnp.repeat(select, 4, axis=1)
    noise_scale = NOISE / math.sqrt(model_width)
    gate_noise = jnp.dot(projected[:, :4 * members] * select, noise_table(member_seeds, 2, expert, hidden_index, expert_count).T, precision=lax.Precision.HIGHEST)
    up_noise = jnp.dot(projected[:, 4 * members:] * select, noise_table(member_seeds, 3, expert, hidden_index, expert_count).T, precision=lax.Precision.HIGHEST)
    gate_sum = jnp.dot(inputs, gate_cols, preferred_element_type=jnp.float32) + noise_scale * gate_noise
    up_sum = jnp.dot(inputs, up_cols, preferred_element_type=jnp.float32) + noise_scale * up_noise
    return (gate_sum * jax.nn.sigmoid(ALPHA * gate_sum) * (up_sum + 1.0)).astype(jnp.bfloat16)

def reference(tokens, routes, router_weight, router_bias, member_seeds, gate_weight, up_weight):
    logits = jnp.dot(tokens, router_weight, preferred_element_type=jnp.float32) + router_bias
    expert_ids = jnp.arange(EXPERTS, dtype=jnp.int32)
    chosen = lax.optimization_barrier(jnp.sum(jnp.where(routes[:, :, None] == expert_ids[None, None, :], logits[:, None, :], 0.0), axis=2))
    weights = jax.nn.softmax(chosen, axis=1)
    flat_routes = routes.reshape(-1)
    entry_count = TOKENS * TOP
    entry_transcript = jnp.arange(entry_count, dtype=jnp.int32) // TOP // LENGTH
    slot_limit = N_EXP * CAP_SEND
    hidden_index = jnp.arange(FW, dtype=jnp.int32)

    def visit_expert(collected, expert):
        is_mine = flat_routes == expert
        entries = jnp.nonzero(is_mine, size=slot_limit, fill_value=entry_count)[0].astype(jnp.int32)
        is_valid = entries < entry_count
        safe_entries = jnp.minimum(entries, entry_count - 1)
        inputs = tokens[safe_entries // TOP]
        transcripts = jnp.where(is_valid, entry_transcript[safe_entries], -1).astype(jnp.int32)
        gate_cols = jnp.concatenate([gate_weight[2 * expert], gate_weight[2 * expert + 1]], axis=1)
        up_cols = jnp.concatenate([up_weight[2 * expert], up_weight[2 * expert + 1]], axis=1)
        activation = expert_rows(inputs, transcripts, member_seeds, gate_cols, up_cols, expert, hidden_index, EXPERTS)
        collected = collected.at[entries].set(activation, mode='drop')
        return (collected, None)
    all_acts = lax.scan(visit_expert, jnp.zeros((entry_count, FW), jnp.bfloat16), expert_ids)[0]
    routed = all_acts.astype(jnp.float32).reshape(TOKENS, TOP, FW) * weights[:, :, None]
    return routed.astype(jnp.bfloat16).reshape(TOKENS, TOP, 2, FW // 2)
```

```python
import functools
import math

import jax
import jax.numpy as jnp
from jax import lax
from jax.experimental import pallas as pl
from jax.experimental.pallas import tpu as pltpu
from jax.sharding import PartitionSpec as P

FW = 1536
LENGTH = 512


NOISE = 0.25
ALPHA = 1.702


def noise_table(member_seeds, matrix_tag, expert, positions, expert_count):
    rank_index = jnp.arange(4, dtype=jnp.int32)
    counter = ((matrix_tag * expert_count + expert) * 4 + rank_index) * 4096
    counter = counter[None, None, :] + positions[:, None, None]
    hashed = (member_seeds[None, :, None] * 31 + counter) * 1103515245 + 12345
    hashed = hashed ^ hashed >> 16
    hashed = hashed * 747796405
    levels = (hashed >> 16 & 255) - 128
    return (levels.astype(jnp.float32) / 128.0).reshape(positions.shape[0], -1)


def expert_rows(
    inputs, transcripts, member_seeds, gate_cols, up_cols, expert, hidden_index, expert_count
):
    model_width = inputs.shape[1]
    members = member_seeds.shape[0]
    positions = jnp.arange(model_width, dtype=jnp.int32)
    left_factors = jnp.concatenate(
        [
            noise_table(member_seeds, 0, expert, positions, expert_count),
            noise_table(member_seeds, 1, expert, positions, expert_count),
        ],
        axis=1,
    ).astype(jnp.bfloat16)
    projected = jnp.dot(inputs, left_factors, preferred_element_type=jnp.float32)
    select = (transcripts[:, None] == jnp.arange(members, dtype=jnp.int32)[None, :]).astype(
        jnp.float32
    )
    select = jnp.repeat(select, 4, axis=1)
    noise_scale = NOISE / math.sqrt(model_width)
    gate_noise = jnp.dot(
        projected[:, : 4 * members] * select,
        noise_table(member_seeds, 2, expert, hidden_index, expert_count).T,
        precision=lax.Precision.HIGHEST,
    )
    up_noise = jnp.dot(
        projected[:, 4 * members :] * select,
        noise_table(member_seeds, 3, expert, hidden_index, expert_count).T,
        precision=lax.Precision.HIGHEST,
    )
    gate_sum = (
        jnp.dot(inputs, gate_cols, preferred_element_type=jnp.float32) + noise_scale * gate_noise
    )
    up_sum = jnp.dot(inputs, up_cols, preferred_element_type=jnp.float32) + noise_scale * up_noise
    return (gate_sum * jax.nn.sigmoid(ALPHA * gate_sum) * (up_sum + 1.0)).astype(jnp.bfloat16)


def local(tokens, routes, router_weight, router_bias, member_seeds, gate_weight, up_weight):
    tok_rows = tokens.shape[0]
    top_count = routes.shape[1]
    expert_count = router_weight.shape[1]
    quarter = gate_weight.shape[2]
    capacity = min(tok_rows, max(2, 2 * tok_rows * top_count // expert_count))
    device_count = lax.axis_size("exp")
    home_index = lax.axis_index("exp")
    core_index = lax.axis_index("tp")
    half_index = home_index % 2
    this_expert = home_index // 2
    partial_logits = jnp.dot(tokens, router_weight, preferred_element_type=jnp.float32)
    logits = lax.psum(partial_logits, "tp") + router_bias
    expert_ids = jnp.arange(expert_count, dtype=jnp.int32)
    chosen = jnp.sum(
        jnp.where(routes[:, :, None] == expert_ids[None, None, :], logits[:, None, :], 0.0), axis=2
    )
    weights = jax.nn.softmax(chosen, axis=1)
    flat_routes = routes.reshape(-1)
    entry_count = tok_rows * top_count
    flat_hot = (flat_routes[:, None] == expert_ids[None, :]).astype(jnp.int32)
    slot_index = jnp.sum((jnp.cumsum(flat_hot, axis=0) - 1) * flat_hot, axis=1)
    entry_rows = jnp.arange(entry_count, dtype=jnp.int32) // top_count
    entry_transcript = ((home_index * tok_rows + entry_rows) // LENGTH).astype(jnp.bfloat16)
    features = lax.all_gather(tokens, "tp", axis=1, tiled=True)
    feature_width = features.shape[1]
    entry_features = features[entry_rows]
    destination = jnp.concatenate([2 * flat_routes, 2 * flat_routes + 1])
    position = jnp.concatenate([slot_index, slot_index])
    payload = jnp.concatenate([entry_features, entry_features], axis=0)
    labels = jnp.concatenate([entry_transcript, entry_transcript])
    target = destination * capacity + position
    send_rows = (
        jnp.zeros((device_count * capacity, feature_width), jnp.bfloat16).at[target].set(payload)
    )
    send_rows = send_rows.reshape(device_count, capacity, feature_width)
    send_labels = jnp.full((device_count * capacity,), -1.0, jnp.bfloat16).at[target].set(labels)
    send_labels = send_labels.reshape(device_count, capacity)
    hidden_index = (
        half_index * (FW // 2) + core_index * quarter + jnp.arange(quarter, dtype=jnp.int32)
    )
    arrived_rows = lax.all_to_all(send_rows, "exp", split_axis=0, concat_axis=0, tiled=True)
    arrived_labels = lax.all_to_all(send_labels, "exp", split_axis=0, concat_axis=0, tiled=True)
    flat_rows = arrived_rows.reshape(-1, arrived_rows.shape[-1])
    transcripts = arrived_labels.reshape(-1).astype(jnp.int32)
    activation = expert_rows(
        flat_rows,
        transcripts,
        member_seeds,
        gate_weight[0],
        up_weight[0],
        this_expert,
        hidden_index,
        expert_count,
    )
    activation = activation.reshape(arrived_labels.shape + (quarter,))
    returned = lax.all_to_all(activation, "exp", split_axis=0, concat_axis=0, tiled=True)
    returned = returned.reshape(-1, quarter)
    pick_index = (
        (2 * flat_routes)[:, None] + jnp.arange(2, dtype=jnp.int32)[None, :]
    ) * capacity + slot_index[:, None]
    picked = returned[pick_index]
    routed = (picked.astype(jnp.float32) * weights.reshape(-1)[:, None, None]).astype(jnp.bfloat16)
    return routed.reshape(tok_rows, top_count, 2, quarter)


Z, X, C = 4, 2, 2
ROW = X * C
MESH = pl.DeviceIdType.MESH


def levels(seeds, counter):
    hashed = (seeds * 31 + counter) * 1103515245 + 12345
    hashed = hashed ^ (hashed >> 16)
    hashed = hashed * 747796405
    return (((hashed >> 16) & 255) - 128).astype(jnp.float32) / 128.0


def row_seeds(seed_ref, member, members):
    seeds = jnp.zeros_like(member)
    for index in range(members):
        seeds = jnp.where(member == index, seed_ref[index], seeds)
    return seeds


def fused(
    expert_count, seed_ref, tokens, routes, router, bias, gate, up, out,
    held, wg, wu, gt, ut, left, act, back, gsend, grecv, rsend, rrecv, wsem,
):
    count = Z * ROW
    rows, width = held.shape[1:]
    hidden = wg.shape[1]
    members = seed_ref.shape[0]
    me = lax.axis_index("exp")
    z, x, c = me // ROW, (me // C) % X, me % C
    expert, half = me // 2, me % 2
    whole = width // 128 * 128
    rest = width - whole
    beside, sibling = me + C * (1 - 2 * x), me + 1 - 2 * c

    load = pltpu.make_async_copy(tokens, held.at[me], wsem.at[0])
    load.start()
    load_g = pltpu.make_async_copy(gate.at[0], wg, wsem.at[1])
    load_g.start()
    load_u = pltpu.make_async_copy(up.at[0], wu, wsem.at[2])
    load_u.start()

    barrier = pltpu.get_barrier_semaphore()

    def greet(k, carry):
        pl.semaphore_signal(
            barrier, inc=1, device_id={"exp": (me + k) % count}, device_id_type=MESH
        )
        return carry

    lax.fori_loop(1, count, greet, 0)
    load.wait()
    pl.semaphore_wait(barrier, count - 1)

    def pass_on(slot, way, target):
        return pltpu.make_async_remote_copy(
            src_ref=held.at[slot], dst_ref=held.at[slot],
            send_sem=gsend.at[slot, way], recv_sem=grecv.at[slot],
            device_id={"exp": target}, device_id_type=MESH,
        )

    def arrived(slot):
        pass_on(slot, 3, sibling).wait_recv()

    def give_back(slot):
        return pltpu.make_async_remote_copy(
            src_ref=act.at[slot], dst_ref=back.at[half, expert],
            send_sem=rsend.at[slot], recv_sem=rrecv.at[me],
            device_id={"exp": slot}, device_id_type=MESH,
        )

    @pl.when(z < Z - 1)
    def _():
        pass_on(me, 0, me + ROW).start()

    @pl.when(z > 0)
    def _():
        pass_on(me, 1, me - ROW).start()

    pass_on(me, 2, beside).start()
    pass_on(me, 3, sibling).start()

    noisy = 8 * members
    k = lax.broadcasted_iota(jnp.int32, (noisy, width), 0)
    i = lax.broadcasted_iota(jnp.int32, (noisy, width), 1)
    seeds = row_seeds(seed_ref, (k // 4) % members, members)
    number = ((k // (4 * members)) * expert_count + expert) * 4 + k % 4
    left[...] = levels(seeds, number * 4096 + i).astype(jnp.bfloat16)
    k = lax.broadcasted_iota(jnp.int32, (noisy, hidden), 0)
    i = lax.broadcasted_iota(jnp.int32, (noisy, hidden), 1) + half * hidden
    seeds = row_seeds(seed_ref, (k // 4) % members, members)
    number = ((2 + k // (4 * members)) * expert_count + expert) * 4 + k % 4
    right = levels(seeds, number * 4096 + i)
    for ref, tag in ((gt, 0), (ut, 1)):
        part = jnp.where(k // (4 * members) == tag, right, 0.0).astype(jnp.bfloat16)
        ref[rest:, :] = jnp.zeros((ref.shape[0] - rest, hidden), jnp.bfloat16)
        for piece in range(3):
            ref[rest + piece * noisy : rest + (piece + 1) * noisy, :] = part
    top = routes.shape[1]
    logits = jnp.dot(held[me], router[...], preferred_element_type=jnp.float32) + bias[...]
    ids = lax.broadcasted_iota(jnp.int32, logits.shape, 1)
    chosen = [
        jnp.sum(jnp.where(routes[:, j : j + 1] == ids, logits, 0.0), axis=1, keepdims=True)
        for j in range(top)
    ]
    peak = functools.reduce(jnp.maximum, chosen)
    grown = [jnp.exp(v - peak) for v in chosen]
    total = sum(grown[1:], grown[0])
    weights = jnp.concatenate([v / total for v in grown], axis=0)
    place = lax.broadcasted_iota(jnp.int32, (rows, expert_count * rows), 1)
    token = lax.broadcasted_iota(jnp.int32, (rows, expert_count * rows), 0)
    pick = jnp.concatenate(
        [
            jnp.where(place == routes[:, j : j + 1] * rows + token, 1.0, 0.0).astype(jnp.bfloat16)
            for j in range(top)
        ],
        axis=0,
    )

    load_g.wait()
    load_u.wait()
    gt[0:rest, :] = wg[whole:, :]
    ut[0:rest, :] = wu[whole:, :]

    scale = NOISE / math.sqrt(width)
    batch = ROW * rows
    tile = 256

    def visit(step, carry):
        above = step + 1

        @pl.when(z - above >= 0)
        def _():
            slot = me - above * ROW
            arrived(slot)

            @pl.when(z < Z - 1)
            def _():
                pass_on(slot, 0, me + ROW).start()

            pass_on(slot, 2, beside).start()
            pass_on(slot, 3, sibling).start()

        @pl.when(z + above < Z)
        def _():
            slot = me + above * ROW
            arrived(slot)

            @pl.when(z > 0)
            def _():
                pass_on(slot, 1, me - ROW).start()

            pass_on(slot, 2, beside).start()
            pass_on(slot, 3, sibling).start()

        mirror = z // 2
        folded = z + mirror * (3 - 2 * z)
        first = 1 - step // 2
        near = first * (folded + (step % 2) * (1 - 2 * folded)) + (1 - first) * step
        row = near + mirror * (3 - 2 * near)
        base = row * ROW
        across = base + (1 - x) * C + c
        arrived(across)
        pass_on(across, 3, sibling).start()

        @pl.when(step == 0)
        def _():
            arrived(sibling)

        @pl.when(step > 0)
        def _():
            arrived(base + x * C + 1 - c)

        arrived(base + (1 - x) * C + 1 - c)

        values = held[pl.ds(base, ROW)].reshape(batch, width)
        projected = lax.dot_general(
            values, left[...], (((1,), (1,)), ((), ())), preferred_element_type=jnp.float32
        )
        where = base * rows + lax.broadcasted_iota(jnp.int32, (batch, noisy), 0)
        member = (lax.broadcasted_iota(jnp.int32, (batch, noisy), 1) // 4) % members
        remaining = jnp.where(where // LENGTH == member, projected * scale, 0.0)
        ends = [values[:, whole:]]
        for _ in range(3):
            piece = remaining.astype(jnp.bfloat16)
            remaining = remaining - piece.astype(jnp.float32)
            ends.append(piece)
        ends.append(jnp.zeros((batch, 128 - rest - 3 * noisy), jnp.bfloat16))
        end = jnp.concatenate(ends, axis=1)

        def columns(n, carry):
            at = pl.ds(pl.multiple_of(n * tile, tile), tile)
            start = held[pl.ds(base, ROW), :, 0:whole].reshape(batch, whole)
            g = jnp.dot(start, wg[0:whole, at], preferred_element_type=jnp.float32)
            g = g + jnp.dot(end, gt[:, at], preferred_element_type=jnp.float32)
            u = jnp.dot(start, wu[0:whole, at], preferred_element_type=jnp.float32)
            u = u + jnp.dot(end, ut[:, at], preferred_element_type=jnp.float32)
            value = (g * jax.nn.sigmoid(ALPHA * g) * (u + 1.0)).astype(jnp.bfloat16)
            act[pl.ds(base, ROW), :, at] = value.reshape(ROW, rows, tile)
            return carry

        lax.fori_loop(0, hidden // tile, columns, 0)
        for other in range(ROW):
            @pl.when(base + other != me)
            def _(slot=base + other):
                give_back(slot).start()
        return carry

    lax.fori_loop(0, Z, visit, 0)
    back[half, expert] = act[me]

    def take(k, carry):
        slot = (me + k) % count
        pltpu.make_async_remote_copy(
            src_ref=act.at[slot], dst_ref=back.at[slot % 2, slot // 2],
            send_sem=rsend.at[slot], recv_sem=rrecv.at[slot],
            device_id={"exp": slot}, device_id_type=MESH,
        ).wait_recv()
        return carry

    lax.fori_loop(1, count, take, 0)
    for h in range(2):
        found = jnp.dot(
            pick, back[h].reshape(expert_count * rows, hidden), preferred_element_type=jnp.float32
        )
        out[:, h * hidden : (h + 1) * hidden] = (found * weights).astype(jnp.bfloat16)

    def sent(k, carry):
        slot = (me + k) % count
        give_back(slot).wait_send()
        return carry

    lax.fori_loop(1, count, sent, 0)

    def passed(zo, carry):
        slot = zo * ROW + x * C + c

        @pl.when((zo <= z) & (z < Z - 1))
        def _():
            pass_on(slot, 0, me + ROW).wait_send()

        @pl.when((zo >= z) & (z > 0))
        def _():
            pass_on(slot, 1, me - ROW).wait_send()

        pass_on(slot, 2, beside).wait_send()
        pass_on(slot, 3, sibling).wait_send()
        pass_on(zo * ROW + (1 - x) * C + c, 3, sibling).wait_send()
        return carry

    lax.fori_loop(0, Z, passed, 0)


def gathered(tokens, routes, router_weight, router_bias, member_seeds, gate_weight, up_weight):
    rows, width = tokens.shape
    top = routes.shape[1]
    expert_count = router_weight.shape[1]
    hidden = gate_weight.shape[2]
    count = Z * ROW
    noisy = 8 * member_seeds.shape[0]
    vmem = pl.BlockSpec(memory_space=pltpu.VMEM)
    anywhere = pl.BlockSpec(memory_space=pl.ANY)
    half_dtype = jnp.bfloat16
    result = pl.pallas_call(
        functools.partial(fused, expert_count),
        out_shape=jax.ShapeDtypeStruct((top * rows, 2 * hidden), half_dtype),
        in_specs=[
            pl.BlockSpec(memory_space=pltpu.SMEM), anywhere, vmem, vmem, vmem, anywhere, anywhere,
        ],
        out_specs=vmem,
        scratch_shapes=[
            pltpu.VMEM((count, rows, width), half_dtype),
            pltpu.VMEM((width, hidden), half_dtype),
            pltpu.VMEM((width, hidden), half_dtype),
            pltpu.VMEM((128, hidden), half_dtype),
            pltpu.VMEM((128, hidden), half_dtype),
            pltpu.VMEM((noisy, width), half_dtype),
            pltpu.VMEM((count, rows, hidden), half_dtype),
            pltpu.VMEM((2, expert_count, rows, hidden), half_dtype),
            pltpu.SemaphoreType.DMA((count, 4)),
            pltpu.SemaphoreType.DMA((count,)),
            pltpu.SemaphoreType.DMA((count,)),
            pltpu.SemaphoreType.DMA((count,)),
            pltpu.SemaphoreType.DMA((3,)),
        ],
        compiler_params=pltpu.CompilerParams(
            collective_id=0, has_side_effects=True, vmem_limit_bytes=48 * 1024 * 1024
        ),
        cost_estimate=pl.CostEstimate(
            flops=4 * count * rows * width * hidden,
            bytes_accessed=4 * width * hidden,
            transcendentals=count * rows * hidden,
        ),
    )(member_seeds, tokens, routes, router_weight, router_bias[None, :], gate_weight, up_weight)
    return result.reshape(top, rows, 2, hidden).transpose(1, 0, 2, 3)


def fits(mesh, tokens, routes, router_weight, member_seeds, gate_weight):
    devices = mesh.shape["exp"]
    rows = tokens.shape[0] // (mesh.shape["pop"] * devices)
    experts = router_weight.shape[1]
    return (
        mesh.shape["tp"] == 1
        and devices == Z * ROW == 2 * experts
        and 2 * rows * routes.shape[1] // experts >= rows
        and tokens.shape[1] % 128 + 24 * (member_seeds.shape[0] // mesh.shape["pop"]) <= 128
        and gate_weight.shape[2] % 256 == 0
    )


def solution(mesh):
    in_specs = (
        P(("pop", "exp"), "tp"),
        P(("pop", "exp"), None),
        P("tp", None),
        P(),
        P("pop"),
        P("exp", None, "tp"),
        P("exp", None, "tp"),
    )
    out_specs = P(("pop", "exp"), None, None, "tp")

    def whole(tokens, routes, router_weight, router_bias, member_seeds, gate_weight, up_weight):
        small = fits(mesh, tokens, routes, router_weight, member_seeds, gate_weight)
        body = gathered if small else local
        return jax.shard_map(
            body, mesh=mesh, in_specs=in_specs, out_specs=out_specs, check_vma=False
        )(tokens, routes, router_weight, router_bias, member_seeds, gate_weight, up_weight)

    return whole
```

```python
import functools
import math

import jax
import jax.numpy as jnp
from jax import lax
from jax.experimental import pallas as pl
from jax.experimental.pallas import tpu as pltpu
from jax.sharding import PartitionSpec as P

FW = 1536
LENGTH = 512


NOISE = 0.25
ALPHA = 1.702


def noise_table(member_seeds, matrix_tag, expert, positions, expert_count):
    rank_index = jnp.arange(4, dtype=jnp.int32)
    counter = ((matrix_tag * expert_count + expert) * 4 + rank_index) * 4096
    counter = counter[None, None, :] + positions[:, None, None]
    hashed = (member_seeds[None, :, None] * 31 + counter) * 1103515245 + 12345
    hashed = hashed ^ hashed >> 16
    hashed = hashed * 747796405
    levels = (hashed >> 16 & 255) - 128
    return (levels.astype(jnp.float32) / 128.0).reshape(positions.shape[0], -1)


def expert_rows(
    inputs, transcripts, member_seeds, gate_cols, up_cols, expert, hidden_index, expert_count
):
    model_width = inputs.shape[1]
    members = member_seeds.shape[0]
    positions = jnp.arange(model_width, dtype=jnp.int32)
    left_factors = jnp.concatenate(
        [
            noise_table(member_seeds, 0, expert, positions, expert_count),
            noise_table(member_seeds, 1, expert, positions, expert_count),
        ],
        axis=1,
    ).astype(jnp.bfloat16)
    projected = jnp.dot(inputs, left_factors, preferred_element_type=jnp.float32)
    select = (transcripts[:, None] == jnp.arange(members, dtype=jnp.int32)[None, :]).astype(
        jnp.float32
    )
    select = jnp.repeat(select, 4, axis=1)
    noise_scale = NOISE / math.sqrt(model_width)
    gate_noise = jnp.dot(
        projected[:, : 4 * members] * select,
        noise_table(member_seeds, 2, expert, hidden_index, expert_count).T,
        precision=lax.Precision.HIGHEST,
    )
    up_noise = jnp.dot(
        projected[:, 4 * members :] * select,
        noise_table(member_seeds, 3, expert, hidden_index, expert_count).T,
        precision=lax.Precision.HIGHEST,
    )
    gate_sum = (
        jnp.dot(inputs, gate_cols, preferred_element_type=jnp.float32) + noise_scale * gate_noise
    )
    up_sum = jnp.dot(inputs, up_cols, preferred_element_type=jnp.float32) + noise_scale * up_noise
    return (gate_sum * jax.nn.sigmoid(ALPHA * gate_sum) * (up_sum + 1.0)).astype(jnp.bfloat16)


def local(tokens, routes, router_weight, router_bias, member_seeds, gate_weight, up_weight):
    tok_rows = tokens.shape[0]
    top_count = routes.shape[1]
    expert_count = router_weight.shape[1]
    quarter = gate_weight.shape[2]
    capacity = min(tok_rows, max(2, 2 * tok_rows * top_count // expert_count))
    device_count = lax.axis_size("exp")
    home_index = lax.axis_index("exp")
    core_index = lax.axis_index("tp")
    half_index = home_index % 2
    this_expert = home_index // 2
    partial_logits = jnp.dot(tokens, router_weight, preferred_element_type=jnp.float32)
    logits = lax.psum(partial_logits, "tp") + router_bias
    expert_ids = jnp.arange(expert_count, dtype=jnp.int32)
    chosen = jnp.sum(
        jnp.where(routes[:, :, None] == expert_ids[None, None, :], logits[:, None, :], 0.0), axis=2
    )
    weights = jax.nn.softmax(chosen, axis=1)
    flat_routes = routes.reshape(-1)
    entry_count = tok_rows * top_count
    flat_hot = (flat_routes[:, None] == expert_ids[None, :]).astype(jnp.int32)
    slot_index = jnp.sum((jnp.cumsum(flat_hot, axis=0) - 1) * flat_hot, axis=1)
    entry_rows = jnp.arange(entry_count, dtype=jnp.int32) // top_count
    entry_transcript = ((home_index * tok_rows + entry_rows) // LENGTH).astype(jnp.bfloat16)
    features = lax.all_gather(tokens, "tp", axis=1, tiled=True)
    feature_width = features.shape[1]
    entry_features = features[entry_rows]
    destination = jnp.concatenate([2 * flat_routes, 2 * flat_routes + 1])
    position = jnp.concatenate([slot_index, slot_index])
    payload = jnp.concatenate([entry_features, entry_features], axis=0)
    labels = jnp.concatenate([entry_transcript, entry_transcript])
    target = destination * capacity + position
    send_rows = (
        jnp.zeros((device_count * capacity, feature_width), jnp.bfloat16).at[target].set(payload)
    )
    send_rows = send_rows.reshape(device_count, capacity, feature_width)
    send_labels = jnp.full((device_count * capacity,), -1.0, jnp.bfloat16).at[target].set(labels)
    send_labels = send_labels.reshape(device_count, capacity)
    hidden_index = (
        half_index * (FW // 2) + core_index * quarter + jnp.arange(quarter, dtype=jnp.int32)
    )
    arrived_rows = lax.all_to_all(send_rows, "exp", split_axis=0, concat_axis=0, tiled=True)
    arrived_labels = lax.all_to_all(send_labels, "exp", split_axis=0, concat_axis=0, tiled=True)
    flat_rows = arrived_rows.reshape(-1, arrived_rows.shape[-1])
    transcripts = arrived_labels.reshape(-1).astype(jnp.int32)
    activation = expert_rows(
        flat_rows,
        transcripts,
        member_seeds,
        gate_weight[0],
        up_weight[0],
        this_expert,
        hidden_index,
        expert_count,
    )
    activation = activation.reshape(arrived_labels.shape + (quarter,))
    returned = lax.all_to_all(activation, "exp", split_axis=0, concat_axis=0, tiled=True)
    returned = returned.reshape(-1, quarter)
    pick_index = (
        (2 * flat_routes)[:, None] + jnp.arange(2, dtype=jnp.int32)[None, :]
    ) * capacity + slot_index[:, None]
    picked = returned[pick_index]
    routed = (picked.astype(jnp.float32) * weights.reshape(-1)[:, None, None]).astype(jnp.bfloat16)
    return routed.reshape(tok_rows, top_count, 2, quarter)


Z, X, C = 4, 2, 2
ROW = X * C
MESH = pl.DeviceIdType.MESH


def levels(seeds, counter):
    hashed = (seeds * 31 + counter) * 1103515245 + 12345
    hashed = hashed ^ (hashed >> 16)
    hashed = hashed * 747796405
    return (((hashed >> 16) & 255) - 128).astype(jnp.float32) / 128.0


def row_seeds(seed_ref, member, members):
    seeds = jnp.zeros_like(member)
    for index in range(members):
        seeds = jnp.where(member == index, seed_ref[index], seeds)
    return seeds


def fused(
    expert_count, seed_hbm, tokens, routes_hbm, router, bias_hbm, gate, up, out,
    seed_ref, routes, bias,
    held, wg, wu, gt, ut, left, act, back, gsend, grecv, rsend, rrecv, wsem,
):
    count = Z * ROW
    rows, width = held.shape[1:]
    hidden = wg.shape[1]
    members = seed_ref.shape[0]
    me = lax.axis_index("exp")
    z, x, c = me // ROW, (me // C) % X, me % C
    expert, half = me // 2, me % 2
    whole = width // 128 * 128
    rest = width - whole
    beside, sibling = me + C * (1 - 2 * x), me + 1 - 2 * c

    load = pltpu.make_async_copy(tokens, held.at[me], wsem.at[0])
    load.start()
    small = [
        pltpu.make_async_copy(source, target, wsem.at[3 + index])
        for index, (source, target) in enumerate(
            [(seed_hbm, seed_ref), (routes_hbm, routes), (bias_hbm, bias)]
        )
    ]
    for copy in small:
        copy.start()
    load_g = pltpu.make_async_copy(gate.at[0], wg, wsem.at[1])
    load_g.start()
    load_u = pltpu.make_async_copy(up.at[0], wu, wsem.at[2])
    load_u.start()

    barrier = pltpu.get_barrier_semaphore()

    def greet(k, carry):
        pl.semaphore_signal(
            barrier, inc=1, device_id={"exp": (me + k) % count}, device_id_type=MESH
        )
        return carry

    lax.fori_loop(1, count, greet, 0)
    load.wait()
    pl.semaphore_wait(barrier, count - 1)

    cut = rows // 2

    def pass_on(slot, piece, way, target):
        block = held.at[slot, pl.ds(piece * cut, cut)]
        return pltpu.make_async_remote_copy(
            src_ref=block, dst_ref=block,
            send_sem=gsend.at[slot, piece, way], recv_sem=grecv.at[slot, piece],
            device_id={"exp": target}, device_id_type=MESH,
        )

    def arrived(slot, piece):
        pass_on(slot, piece, 3, sibling).wait_recv()

    def give_back(slot):
        return pltpu.make_async_remote_copy(
            src_ref=act.at[slot], dst_ref=back.at[half, expert],
            send_sem=rsend.at[slot], recv_sem=rrecv.at[me],
            device_id={"exp": slot}, device_id_type=MESH,
        )

    for piece in range(2):
        @pl.when(z < Z - 1)
        def _(piece=piece):
            pass_on(me, piece, 0, me + ROW).start()

        @pl.when(z > 0)
        def _(piece=piece):
            pass_on(me, piece, 1, me - ROW).start()

        pass_on(me, piece, 2, beside).start()
        pass_on(me, piece, 3, sibling).start()

    def chip_row(step):
        mirror = z // 2
        near = (z + mirror * (3 - 2 * z) + step) % Z
        return near + mirror * (3 - 2 * near)

    def relay(step, piece):
        above = step + 1

        @pl.when(z - above >= 0)
        def _():
            slot = me - above * ROW
            arrived(slot, piece)

            @pl.when(z < Z - 1)
            def _():
                pass_on(slot, piece, 0, me + ROW).start()

            @pl.when(z != 1)
            def _():
                pass_on(slot, piece, 2, beside).start()

            pass_on(slot, piece, 3, sibling).start()

        @pl.when(z + above < Z)
        def _():
            slot = me + above * ROW
            arrived(slot, piece)

            @pl.when(z > 0)
            def _():
                pass_on(slot, piece, 1, me - ROW).start()

            @pl.when(z != Z - 2)
            def _():
                pass_on(slot, piece, 2, beside).start()

            pass_on(slot, piece, 3, sibling).start()

        @pl.when((above == 2) & (z == 1))
        def _():
            pass_on(me - ROW, piece, 2, beside).start()

        @pl.when((above == 2) & (z == Z - 2))
        def _():
            pass_on(me + ROW, piece, 2, beside).start()

        across = chip_row(step) * ROW + (1 - x) * C + c
        arrived(across, piece)
        pass_on(across, piece, 3, sibling).start()

    for copy in small:
        copy.wait()
    noisy = 8 * members
    k = lax.broadcasted_iota(jnp.int32, (noisy, width), 0)
    i = lax.broadcasted_iota(jnp.int32, (noisy, width), 1)
    seeds = row_seeds(seed_ref, (k // 4) % members, members)
    number = ((k // (4 * members)) * expert_count + expert) * 4 + k % 4
    left[...] = levels(seeds, number * 4096 + i).astype(jnp.bfloat16)
    k = lax.broadcasted_iota(jnp.int32, (noisy, hidden), 0)
    i = lax.broadcasted_iota(jnp.int32, (noisy, hidden), 1) + half * hidden
    seeds = row_seeds(seed_ref, (k // 4) % members, members)
    number = ((2 + k // (4 * members)) * expert_count + expert) * 4 + k % 4
    right = levels(seeds, number * 4096 + i)
    for ref, tag in ((gt, 0), (ut, 1)):
        part = jnp.where(k // (4 * members) == tag, right, 0.0).astype(jnp.bfloat16)
        ref[rest:, :] = jnp.zeros((ref.shape[0] - rest, hidden), jnp.bfloat16)
        for piece in range(3):
            ref[rest + piece * noisy : rest + (piece + 1) * noisy, :] = part
    relay(0, 0)
    load_g.wait()
    load_u.wait()
    gt[0:rest, :] = wg[whole:, :]
    ut[0:rest, :] = wu[whole:, :]

    scale = NOISE / math.sqrt(width)
    batch = ROW * rows
    tile = 256

    def visit(step, carry):
        @pl.when(step > 0)
        def _():
            relay(step, 0)

        relay(step, 1)
        base = chip_row(step) * ROW
        for piece in range(2):
            arrived(base + x * C + 1 - c, piece)
            arrived(base + (1 - x) * C + 1 - c, piece)
        values = held[pl.ds(base, ROW)].reshape(batch, width)
        projected = lax.dot_general(
            values, left[...], (((1,), (1,)), ((), ())), preferred_element_type=jnp.float32
        )
        where = base * rows + lax.broadcasted_iota(jnp.int32, (batch, noisy), 0)
        member = (lax.broadcasted_iota(jnp.int32, (batch, noisy), 1) // 4) % members
        remaining = jnp.where(where // LENGTH == member, projected * scale, 0.0)
        ends = [values[:, whole:]]
        for _ in range(3):
            piece = remaining.astype(jnp.bfloat16)
            remaining = remaining - piece.astype(jnp.float32)
            ends.append(piece)
        ends.append(jnp.zeros((batch, 128 - rest - 3 * noisy), jnp.bfloat16))
        end = jnp.concatenate(ends, axis=1)

        def columns(n, carry):
            at = pl.ds(pl.multiple_of(n * tile, tile), tile)
            start = held[pl.ds(base, ROW), :, 0:whole].reshape(batch, whole)
            g = jnp.dot(start, wg[0:whole, at], preferred_element_type=jnp.float32)
            g = g + jnp.dot(end, gt[:, at], preferred_element_type=jnp.float32)
            u = jnp.dot(start, wu[0:whole, at], preferred_element_type=jnp.float32)
            u = u + jnp.dot(end, ut[:, at], preferred_element_type=jnp.float32)
            value = (g * jax.nn.sigmoid(ALPHA * g) * (u + 1.0)).astype(jnp.bfloat16)
            act[pl.ds(base, ROW), :, at] = value.reshape(ROW, rows, tile)
            return carry

        lax.fori_loop(0, hidden // tile, columns, 0)

        @pl.when(step > 0)
        def _():
            for other in range(ROW):
                give_back(base + other).start()
        return carry

    lax.fori_loop(0, Z, visit, 0)
    give_back(beside).start()
    give_back(beside + 1 - 2 * c).start()
    give_back(sibling).start()
    back[half, expert] = act[me]

    top = routes.shape[0]
    logits = lax.dot_general(
        held[me], router[...], (((1,), (1,)), ((), ())), preferred_element_type=jnp.float32
    )
    logits = logits + bias[...]
    ids = lax.broadcasted_iota(jnp.int32, logits.shape, 1).astype(jnp.float32)
    line = lax.broadcasted_iota(jnp.int32, (rows, rows), 0)
    unit = jnp.where(line == lax.broadcasted_iota(jnp.int32, (rows, rows), 1), 1.0, 0.0)
    named = lax.dot_general(
        unit.astype(jnp.bfloat16), routes[...].astype(jnp.float32).astype(jnp.bfloat16),
        (((1,), (1,)), ((), ())), preferred_element_type=jnp.float32,
    )
    chosen = [
        jnp.sum(jnp.where(named[:, j : j + 1] == ids, logits, 0.0), axis=1, keepdims=True)
        for j in range(top)
    ]
    peak = functools.reduce(jnp.maximum, chosen)
    grown = [jnp.exp(v - peak) for v in chosen]
    total = sum(grown[1:], grown[0])
    weights = jnp.concatenate([v / total for v in grown], axis=0)
    place = lax.broadcasted_iota(jnp.int32, (rows, expert_count * rows), 1).astype(jnp.float32)
    token = lax.broadcasted_iota(jnp.int32, (rows, expert_count * rows), 0).astype(jnp.float32)
    pick = jnp.concatenate(
        [
            jnp.where(place == named[:, j : j + 1] * rows + token, 1.0, 0.0).astype(jnp.bfloat16)
            for j in range(top)
        ],
        axis=0,
    )

    def take(k, carry):
        slot = (me + k) % count
        pltpu.make_async_remote_copy(
            src_ref=act.at[slot], dst_ref=back.at[slot % 2, slot // 2],
            send_sem=rsend.at[slot], recv_sem=rrecv.at[slot],
            device_id={"exp": slot}, device_id_type=MESH,
        ).wait_recv()
        return carry

    lax.fori_loop(1, count, take, 0)
    for h in range(2):
        found = jnp.dot(
            pick, back[h].reshape(expert_count * rows, hidden), preferred_element_type=jnp.float32
        )
        out[:, h * hidden : (h + 1) * hidden] = (found * weights).astype(jnp.bfloat16)

    def sent(k, carry):
        slot = (me + k) % count
        give_back(slot).wait_send()
        return carry

    lax.fori_loop(1, count, sent, 0)

    def passed(k, carry):
        zo, piece = k // 2, k % 2
        slot = zo * ROW + x * C + c

        @pl.when((zo <= z) & (z < Z - 1))
        def _():
            pass_on(slot, piece, 0, me + ROW).wait_send()

        @pl.when((zo >= z) & (z > 0))
        def _():
            pass_on(slot, piece, 1, me - ROW).wait_send()

        pass_on(slot, piece, 2, beside).wait_send()
        pass_on(slot, piece, 3, sibling).wait_send()
        pass_on(zo * ROW + (1 - x) * C + c, piece, 3, sibling).wait_send()
        return carry

    lax.fori_loop(0, 2 * Z, passed, 0)


def gathered(tokens, routes, router_weight, router_bias, member_seeds, gate_weight, up_weight):
    rows, width = tokens.shape
    top = routes.shape[1]
    expert_count = router_weight.shape[1]
    hidden = gate_weight.shape[2]
    count = Z * ROW
    noisy = 8 * member_seeds.shape[0]
    vmem = pl.BlockSpec(memory_space=pltpu.VMEM)
    anywhere = pl.BlockSpec(memory_space=pl.ANY)
    half_dtype = jnp.bfloat16
    result = pl.pallas_call(
        functools.partial(fused, expert_count),
        out_shape=jax.ShapeDtypeStruct((top * rows, 2 * hidden), half_dtype),
        in_specs=[anywhere] * 3 + [vmem] + [anywhere] * 3,
        out_specs=vmem,
        scratch_shapes=[
            pltpu.SMEM(member_seeds.shape, jnp.int32),
            pltpu.VMEM((top, rows), jnp.int32),
            pltpu.VMEM((1, expert_count), jnp.float32),
            pltpu.VMEM((count, rows, width), half_dtype),
            pltpu.VMEM((width, hidden), half_dtype),
            pltpu.VMEM((width, hidden), half_dtype),
            pltpu.VMEM((128, hidden), half_dtype),
            pltpu.VMEM((128, hidden), half_dtype),
            pltpu.VMEM((noisy, width), half_dtype),
            pltpu.VMEM((count, rows, hidden), half_dtype),
            pltpu.VMEM((2, expert_count, rows, hidden), half_dtype),
            pltpu.SemaphoreType.DMA((count, 2, 4)),
            pltpu.SemaphoreType.DMA((count, 2)),
            pltpu.SemaphoreType.DMA((count,)),
            pltpu.SemaphoreType.DMA((count,)),
            pltpu.SemaphoreType.DMA((6,)),
        ],
        compiler_params=pltpu.CompilerParams(
            collective_id=0, has_side_effects=True, vmem_limit_bytes=60 * 1024 * 1024
        ),
        cost_estimate=pl.CostEstimate(
            flops=4 * count * rows * width * hidden,
            bytes_accessed=4 * width * hidden,
            transcendentals=count * rows * hidden,
        ),
    )(
        member_seeds, tokens, routes.T, router_weight.T, router_bias[None, :], gate_weight, up_weight
    )
    return result.reshape(top, rows, 2, hidden).transpose(1, 0, 2, 3)


def fits(mesh, tokens, routes, router_weight, member_seeds, gate_weight):
    devices = mesh.shape["exp"]
    rows = tokens.shape[0] // (mesh.shape["pop"] * devices)
    experts = router_weight.shape[1]
    return (
        mesh.shape["tp"] == 1
        and devices == Z * ROW == 2 * experts
        and 2 * rows * routes.shape[1] // experts >= rows
        and tokens.shape[1] % 128 + 24 * (member_seeds.shape[0] // mesh.shape["pop"]) <= 128
        and gate_weight.shape[2] % 256 == 0
    )


def solution(mesh):
    in_specs = (
        P(("pop", "exp"), "tp"),
        P(("pop", "exp"), None),
        P("tp", None),
        P(),
        P("pop"),
        P("exp", None, "tp"),
        P("exp", None, "tp"),
    )
    out_specs = P(("pop", "exp"), None, None, "tp")

    def whole(tokens, routes, router_weight, router_bias, member_seeds, gate_weight, up_weight):
        small = fits(mesh, tokens, routes, router_weight, member_seeds, gate_weight)
        body = gathered if small else local
        return jax.shard_map(
            body, mesh=mesh, in_specs=in_specs, out_specs=out_specs, check_vma=False
        )(tokens, routes, router_weight, router_bias, member_seeds, gate_weight, up_weight)

    return whole
```

```python
import functools
import math

import jax
import jax.numpy as jnp
from jax import lax
from jax.experimental import pallas as pl
from jax.experimental.pallas import tpu as pltpu
from jax.sharding import PartitionSpec as P

FW = 1536
LENGTH = 512


NOISE = 0.25
ALPHA = 1.702


def noise_table(member_seeds, matrix_tag, expert, positions, expert_count):
    rank_index = jnp.arange(4, dtype=jnp.int32)
    counter = ((matrix_tag * expert_count + expert) * 4 + rank_index) * 4096
    counter = counter[None, None, :] + positions[:, None, None]
    hashed = (member_seeds[None, :, None] * 31 + counter) * 1103515245 + 12345
    hashed = hashed ^ hashed >> 16
    hashed = hashed * 747796405
    levels = (hashed >> 16 & 255) - 128
    return (levels.astype(jnp.float32) / 128.0).reshape(positions.shape[0], -1)


def expert_rows(
    inputs, transcripts, member_seeds, gate_cols, up_cols, expert, hidden_index, expert_count
):
    model_width = inputs.shape[1]
    members = member_seeds.shape[0]
    positions = jnp.arange(model_width, dtype=jnp.int32)
    left_factors = jnp.concatenate(
        [
            noise_table(member_seeds, 0, expert, positions, expert_count),
            noise_table(member_seeds, 1, expert, positions, expert_count),
        ],
        axis=1,
    ).astype(jnp.bfloat16)
    projected = jnp.dot(inputs, left_factors, preferred_element_type=jnp.float32)
    select = (transcripts[:, None] == jnp.arange(members, dtype=jnp.int32)[None, :]).astype(
        jnp.float32
    )
    select = jnp.repeat(select, 4, axis=1)
    noise_scale = NOISE / math.sqrt(model_width)
    gate_noise = jnp.dot(
        projected[:, : 4 * members] * select,
        noise_table(member_seeds, 2, expert, hidden_index, expert_count).T,
        precision=lax.Precision.HIGHEST,
    )
    up_noise = jnp.dot(
        projected[:, 4 * members :] * select,
        noise_table(member_seeds, 3, expert, hidden_index, expert_count).T,
        precision=lax.Precision.HIGHEST,
    )
    gate_sum = (
        jnp.dot(inputs, gate_cols, preferred_element_type=jnp.float32) + noise_scale * gate_noise
    )
    up_sum = jnp.dot(inputs, up_cols, preferred_element_type=jnp.float32) + noise_scale * up_noise
    return (gate_sum * jax.nn.sigmoid(ALPHA * gate_sum) * (up_sum + 1.0)).astype(jnp.bfloat16)


def local(tokens, routes, router_weight, router_bias, member_seeds, gate_weight, up_weight):
    tok_rows = tokens.shape[0]
    top_count = routes.shape[1]
    expert_count = router_weight.shape[1]
    quarter = gate_weight.shape[2]
    capacity = min(tok_rows, max(2, 2 * tok_rows * top_count // expert_count))
    device_count = lax.axis_size("exp")
    home_index = lax.axis_index("exp")
    core_index = lax.axis_index("tp")
    half_index = home_index % 2
    this_expert = home_index // 2
    partial_logits = jnp.dot(tokens, router_weight, preferred_element_type=jnp.float32)
    logits = lax.psum(partial_logits, "tp") + router_bias
    expert_ids = jnp.arange(expert_count, dtype=jnp.int32)
    chosen = jnp.sum(
        jnp.where(routes[:, :, None] == expert_ids[None, None, :], logits[:, None, :], 0.0), axis=2
    )
    weights = jax.nn.softmax(chosen, axis=1)
    flat_routes = routes.reshape(-1)
    entry_count = tok_rows * top_count
    flat_hot = (flat_routes[:, None] == expert_ids[None, :]).astype(jnp.int32)
    slot_index = jnp.sum((jnp.cumsum(flat_hot, axis=0) - 1) * flat_hot, axis=1)
    entry_rows = jnp.arange(entry_count, dtype=jnp.int32) // top_count
    entry_transcript = ((home_index * tok_rows + entry_rows) // LENGTH).astype(jnp.bfloat16)
    features = lax.all_gather(tokens, "tp", axis=1, tiled=True)
    feature_width = features.shape[1]
    entry_features = features[entry_rows]
    destination = jnp.concatenate([2 * flat_routes, 2 * flat_routes + 1])
    position = jnp.concatenate([slot_index, slot_index])
    payload = jnp.concatenate([entry_features, entry_features], axis=0)
    labels = jnp.concatenate([entry_transcript, entry_transcript])
    target = destination * capacity + position
    send_rows = (
        jnp.zeros((device_count * capacity, feature_width), jnp.bfloat16).at[target].set(payload)
    )
    send_rows = send_rows.reshape(device_count, capacity, feature_width)
    send_labels = jnp.full((device_count * capacity,), -1.0, jnp.bfloat16).at[target].set(labels)
    send_labels = send_labels.reshape(device_count, capacity)
    hidden_index = (
        half_index * (FW // 2) + core_index * quarter + jnp.arange(quarter, dtype=jnp.int32)
    )
    arrived_rows = lax.all_to_all(send_rows, "exp", split_axis=0, concat_axis=0, tiled=True)
    arrived_labels = lax.all_to_all(send_labels, "exp", split_axis=0, concat_axis=0, tiled=True)
    flat_rows = arrived_rows.reshape(-1, arrived_rows.shape[-1])
    transcripts = arrived_labels.reshape(-1).astype(jnp.int32)
    activation = expert_rows(
        flat_rows,
        transcripts,
        member_seeds,
        gate_weight[0],
        up_weight[0],
        this_expert,
        hidden_index,
        expert_count,
    )
    activation = activation.reshape(arrived_labels.shape + (quarter,))
    returned = lax.all_to_all(activation, "exp", split_axis=0, concat_axis=0, tiled=True)
    returned = returned.reshape(-1, quarter)
    pick_index = (
        (2 * flat_routes)[:, None] + jnp.arange(2, dtype=jnp.int32)[None, :]
    ) * capacity + slot_index[:, None]
    picked = returned[pick_index]
    routed = (picked.astype(jnp.float32) * weights.reshape(-1)[:, None, None]).astype(jnp.bfloat16)
    return routed.reshape(tok_rows, top_count, 2, quarter)


Z, X, C = 4, 2, 2
PIECES = 2
ROW = X * C
MESH = pl.DeviceIdType.MESH


def levels(seeds, counter):
    hashed = (seeds * 31 + counter) * 1103515245 + 12345
    hashed = hashed ^ (hashed >> 16)
    hashed = hashed * 747796405
    return (((hashed >> 16) & 255) - 128).astype(jnp.float32) / 128.0


def row_seeds(seed_ref, member, members):
    seeds = jnp.zeros_like(member)
    for index in range(members):
        seeds = jnp.where(member == index, seed_ref[index], seeds)
    return seeds


def fused(
    expert_count, seed_hbm, tokens, routes_hbm, router, bias_hbm, gate, up, out,
    seed_ref, routes, bias,
    held, wg, wu, gt, ut, left, act, back, gsend, grecv, rsend, rrecv, wsem,
):
    count = Z * ROW
    rows, width = held.shape[1:]
    hidden = wg.shape[1]
    members = seed_ref.shape[0]
    me = lax.axis_index("exp")
    z, x, c = me // ROW, (me // C) % X, me % C
    expert, half = me // 2, me % 2
    whole = width // 128 * 128
    rest = width - whole
    beside, sibling = me + C * (1 - 2 * x), me + 1 - 2 * c

    load = pltpu.make_async_copy(tokens, held.at[me], wsem.at[0])
    load.start()
    small = [
        pltpu.make_async_copy(source, target, wsem.at[3 + index])
        for index, (source, target) in enumerate(
            [(seed_hbm, seed_ref), (routes_hbm, routes), (bias_hbm, bias)]
        )
    ]
    for copy in small:
        copy.start()
    load_g = pltpu.make_async_copy(gate.at[0], wg, wsem.at[1])
    load_g.start()
    load_u = pltpu.make_async_copy(up.at[0], wu, wsem.at[2])
    load_u.start()

    barrier = pltpu.get_barrier_semaphore()

    def greet(k, carry):
        pl.semaphore_signal(
            barrier, inc=1, device_id={"exp": (me + k) % count}, device_id_type=MESH
        )
        return carry

    lax.fori_loop(1, count, greet, 0)
    load.wait()
    pl.semaphore_wait(barrier, count - 1)

    cut = rows // PIECES

    def pass_on(slot, piece, way, target):
        block = held.at[slot, pl.ds(piece * cut, cut)]
        return pltpu.make_async_remote_copy(
            src_ref=block, dst_ref=block,
            send_sem=gsend.at[slot, piece, way], recv_sem=grecv.at[slot, piece],
            device_id={"exp": target}, device_id_type=MESH,
        )

    def arrived(slot, piece):
        pass_on(slot, piece, 3, sibling).wait_recv()

    def give_back(slot):
        return pltpu.make_async_remote_copy(
            src_ref=act.at[slot], dst_ref=back.at[half, expert],
            send_sem=rsend.at[slot], recv_sem=rrecv.at[me],
            device_id={"exp": slot}, device_id_type=MESH,
        )

    for piece in range(PIECES):
        @pl.when(z < Z - 1)
        def _(piece=piece):
            pass_on(me, piece, 0, me + ROW).start()

        @pl.when(z > 0)
        def _(piece=piece):
            pass_on(me, piece, 1, me - ROW).start()

        pass_on(me, piece, 2, beside).start()
        pass_on(me, piece, 3, sibling).start()

    def chip_row(step):
        mirror = z // 2
        near = (z + mirror * (3 - 2 * z) + step) % Z
        return near + mirror * (3 - 2 * near)

    def relay(step, piece):
        above = step + 1

        @pl.when(z - above >= 0)
        def _():
            slot = me - above * ROW
            arrived(slot, piece)

            @pl.when(z < Z - 1)
            def _():
                pass_on(slot, piece, 0, me + ROW).start()

            @pl.when(z != 1)
            def _():
                pass_on(slot, piece, 2, beside).start()

            pass_on(slot, piece, 3, sibling).start()

        @pl.when(z + above < Z)
        def _():
            slot = me + above * ROW
            arrived(slot, piece)

            @pl.when(z > 0)
            def _():
                pass_on(slot, piece, 1, me - ROW).start()

            @pl.when(z != Z - 2)
            def _():
                pass_on(slot, piece, 2, beside).start()

            pass_on(slot, piece, 3, sibling).start()

        across = chip_row(step) * ROW + (1 - x) * C + c
        arrived(across, piece)
        pass_on(across, piece, 3, sibling).start()

        @pl.when((step == 0) & (z == 0))
        def _():
            pass_on(across, piece, 0, me + ROW).start()

        @pl.when((step == 0) & (z == Z - 1))
        def _():
            pass_on(across, piece, 1, me - ROW).start()

    for copy in small:
        copy.wait()
    noisy = 8 * members
    k = lax.broadcasted_iota(jnp.int32, (noisy, width), 0)
    i = lax.broadcasted_iota(jnp.int32, (noisy, width), 1)
    seeds = row_seeds(seed_ref, (k // 4) % members, members)
    number = ((k // (4 * members)) * expert_count + expert) * 4 + k % 4
    left[...] = levels(seeds, number * 4096 + i).astype(jnp.bfloat16)
    k = lax.broadcasted_iota(jnp.int32, (noisy, hidden), 0)
    i = lax.broadcasted_iota(jnp.int32, (noisy, hidden), 1) + half * hidden
    seeds = row_seeds(seed_ref, (k // 4) % members, members)
    number = ((2 + k // (4 * members)) * expert_count + expert) * 4 + k % 4
    right = levels(seeds, number * 4096 + i)
    for ref, tag in ((gt, 0), (ut, 1)):
        part = jnp.where(k // (4 * members) == tag, right, 0.0).astype(jnp.bfloat16)
        ref[rest:, :] = jnp.zeros((ref.shape[0] - rest, hidden), jnp.bfloat16)
        for piece in range(3):
            ref[rest + piece * noisy : rest + (piece + 1) * noisy, :] = part
    load_g.wait()
    load_u.wait()
    gt[0:rest, :] = wg[whole:, :]
    ut[0:rest, :] = wu[whole:, :]

    scale = NOISE / math.sqrt(width)
    batch = C * rows
    tile = 256

    def compute(base):
        values = held[pl.ds(base, C)].reshape(batch, width)
        projected = lax.dot_general(
            values, left[...], (((1,), (1,)), ((), ())), preferred_element_type=jnp.float32
        )
        where = base * rows + lax.broadcasted_iota(jnp.int32, (batch, noisy), 0)
        member = (lax.broadcasted_iota(jnp.int32, (batch, noisy), 1) // 4) % members
        remaining = jnp.where(where // LENGTH == member, projected * scale, 0.0)
        ends = [values[:, whole:]]
        for _ in range(3):
            piece = remaining.astype(jnp.bfloat16)
            remaining = remaining - piece.astype(jnp.float32)
            ends.append(piece)
        ends.append(jnp.zeros((batch, 128 - rest - 3 * noisy), jnp.bfloat16))
        end = jnp.concatenate(ends, axis=1)

        def columns(n, carry):
            at = pl.ds(pl.multiple_of(n * tile, tile), tile)
            start = held[pl.ds(base, C), :, 0:whole].reshape(batch, whole)
            g = jnp.dot(start, wg[0:whole, at], preferred_element_type=jnp.float32)
            g = g + jnp.dot(end, gt[:, at], preferred_element_type=jnp.float32)
            u = jnp.dot(start, wu[0:whole, at], preferred_element_type=jnp.float32)
            u = u + jnp.dot(end, ut[:, at], preferred_element_type=jnp.float32)
            value = (g * jax.nn.sigmoid(ALPHA * g) * (u + 1.0)).astype(jnp.bfloat16)
            act[pl.ds(base, C), :, at] = value.reshape(C, rows, tile)
            return carry

        lax.fori_loop(0, hidden // tile, columns, 0)

    def column(row):
        @pl.when((row >= 0) & (row < Z))
        def _():
            base = row * ROW + x * C
            for piece in range(PIECES):
                arrived(base + 1 - c, piece)
            compute(base)
            for other in range(C):
                give_back(base + other).start()

    def visit(step, carry):
        def forward(piece, carry):
            relay(step, piece)
            return carry

        lax.fori_loop(0, PIECES, forward, 0)
        inward = 1 - 2 * (z // 2)
        column(z + inward * (step + 1))
        column(z - inward * (step + 1))
        base = chip_row(step) * ROW + (1 - x) * C
        for piece in range(PIECES):
            arrived(base + 1 - c, piece)
        compute(base)
        return carry

    for piece in range(PIECES):
        arrived(sibling, piece)
    compute(me - c)
    lax.fori_loop(0, Z, visit, 0)
    def far(step):
        for other in range(C):
            give_back(chip_row(step) * ROW + (1 - x) * C + other).start()

    middle = (z // 2 + z) % 2

    @pl.when(middle == 0)
    def _():
        for step in (3, 2, 1):
            far(step)

    @pl.when(middle == 1)
    def _():
        for step in (2, 1, 3):
            far(step)

    give_back(beside).start()
    give_back(beside + 1 - 2 * c).start()
    give_back(sibling).start()
    back[half, expert] = act[me]

    top = routes.shape[0]
    logits = lax.dot_general(
        held[me], router[...], (((1,), (1,)), ((), ())), preferred_element_type=jnp.float32
    )
    logits = logits + bias[...]
    ids = lax.broadcasted_iota(jnp.int32, logits.shape, 1).astype(jnp.float32)
    line = lax.broadcasted_iota(jnp.int32, (rows, rows), 0)
    unit = jnp.where(line == lax.broadcasted_iota(jnp.int32, (rows, rows), 1), 1.0, 0.0)
    named = lax.dot_general(
        unit.astype(jnp.bfloat16), routes[...].astype(jnp.float32).astype(jnp.bfloat16),
        (((1,), (1,)), ((), ())), preferred_element_type=jnp.float32,
    )
    chosen = [
        jnp.sum(jnp.where(named[:, j : j + 1] == ids, logits, 0.0), axis=1, keepdims=True)
        for j in range(top)
    ]
    peak = functools.reduce(jnp.maximum, chosen)
    grown = [jnp.exp(v - peak) for v in chosen]
    total = sum(grown[1:], grown[0])
    weights = jnp.concatenate([v / total for v in grown], axis=0)
    place = lax.broadcasted_iota(jnp.int32, (rows, expert_count * rows), 1).astype(jnp.float32)
    token = lax.broadcasted_iota(jnp.int32, (rows, expert_count * rows), 0).astype(jnp.float32)
    pick = jnp.concatenate(
        [
            jnp.where(place == named[:, j : j + 1] * rows + token, 1.0, 0.0).astype(jnp.bfloat16)
            for j in range(top)
        ],
        axis=0,
    )

    def take(k, carry):
        slot = (me + k) % count
        pltpu.make_async_remote_copy(
            src_ref=act.at[slot], dst_ref=back.at[slot % 2, slot // 2],
            send_sem=rsend.at[slot], recv_sem=rrecv.at[slot],
            device_id={"exp": slot}, device_id_type=MESH,
        ).wait_recv()
        return carry

    lax.fori_loop(1, count, take, 0)
    for h in range(2):
        found = jnp.dot(
            pick, back[h].reshape(expert_count * rows, hidden), preferred_element_type=jnp.float32
        )
        out[:, h * hidden : (h + 1) * hidden] = (found * weights).astype(jnp.bfloat16)

    def sent(k, carry):
        slot = (me + k) % count
        give_back(slot).wait_send()
        return carry

    lax.fori_loop(1, count, sent, 0)

    def passed(k, carry):
        zo, piece = k // PIECES, k % PIECES
        slot = zo * ROW + x * C + c

        @pl.when((zo <= z) & (z < Z - 1))
        def _():
            pass_on(slot, piece, 0, me + ROW).wait_send()

        @pl.when((zo >= z) & (z > 0))
        def _():
            pass_on(slot, piece, 1, me - ROW).wait_send()

        @pl.when(((z != 1) | (zo != 0)) & ((z != Z - 2) | (zo != Z - 1)))
        def _():
            pass_on(slot, piece, 2, beside).wait_send()

        @pl.when((zo == 0) & (z == 0))
        def _():
            pass_on(zo * ROW + (1 - x) * C + c, piece, 0, me + ROW).wait_send()

        @pl.when((zo == Z - 1) & (z == Z - 1))
        def _():
            pass_on(zo * ROW + (1 - x) * C + c, piece, 1, me - ROW).wait_send()

        pass_on(slot, piece, 3, sibling).wait_send()
        pass_on(zo * ROW + (1 - x) * C + c, piece, 3, sibling).wait_send()
        return carry

    lax.fori_loop(0, PIECES * Z, passed, 0)


def gathered(tokens, routes, router_weight, router_bias, member_seeds, gate_weight, up_weight):
    rows, width = tokens.shape
    top = routes.shape[1]
    expert_count = router_weight.shape[1]
    hidden = gate_weight.shape[2]
    count = Z * ROW
    noisy = 8 * member_seeds.shape[0]
    vmem = pl.BlockSpec(memory_space=pltpu.VMEM)
    anywhere = pl.BlockSpec(memory_space=pl.ANY)
    half_dtype = jnp.bfloat16
    result = pl.pallas_call(
        functools.partial(fused, expert_count),
        out_shape=jax.ShapeDtypeStruct((top * rows, 2 * hidden), half_dtype),
        in_specs=[anywhere] * 3 + [vmem] + [anywhere] * 3,
        out_specs=vmem,
        scratch_shapes=[
            pltpu.SMEM(member_seeds.shape, jnp.int32),
            pltpu.VMEM((top, rows), jnp.int32),
            pltpu.VMEM((1, expert_count), jnp.float32),
            pltpu.VMEM((count, rows, width), half_dtype),
            pltpu.VMEM((width, hidden), half_dtype),
            pltpu.VMEM((width, hidden), half_dtype),
            pltpu.VMEM((128, hidden), half_dtype),
            pltpu.VMEM((128, hidden), half_dtype),
            pltpu.VMEM((noisy, width), half_dtype),
            pltpu.VMEM((count, rows, hidden), half_dtype),
            pltpu.VMEM((2, expert_count, rows, hidden), half_dtype),
            pltpu.SemaphoreType.DMA((count, PIECES, 4)),
            pltpu.SemaphoreType.DMA((count, PIECES)),
            pltpu.SemaphoreType.DMA((count,)),
            pltpu.SemaphoreType.DMA((count,)),
            pltpu.SemaphoreType.DMA((6,)),
        ],
        compiler_params=pltpu.CompilerParams(
            collective_id=0, has_side_effects=True, vmem_limit_bytes=60 * 1024 * 1024
        ),
        cost_estimate=pl.CostEstimate(
            flops=4 * count * rows * width * hidden,
            bytes_accessed=4 * width * hidden,
            transcendentals=count * rows * hidden,
        ),
    )(
        member_seeds, tokens, routes.T, router_weight.T, router_bias[None, :], gate_weight, up_weight
    )
    return result.reshape(top, rows, 2, hidden).transpose(1, 0, 2, 3)


def fits(mesh, tokens, routes, router_weight, member_seeds, gate_weight):
    devices = mesh.shape["exp"]
    rows = tokens.shape[0] // (mesh.shape["pop"] * devices)
    experts = router_weight.shape[1]
    return (
        mesh.shape["tp"] == 1
        and devices == Z * ROW == 2 * experts
        and 2 * rows * routes.shape[1] // experts >= rows
        and tokens.shape[1] % 128 + 24 * (member_seeds.shape[0] // mesh.shape["pop"]) <= 128
        and gate_weight.shape[2] % 256 == 0
    )


def solution(mesh):
    in_specs = (
        P(("pop", "exp"), "tp"),
        P(("pop", "exp"), None),
        P("tp", None),
        P(),
        P("pop"),
        P("exp", None, "tp"),
        P("exp", None, "tp"),
    )
    out_specs = P(("pop", "exp"), None, None, "tp")

    def whole(tokens, routes, router_weight, router_bias, member_seeds, gate_weight, up_weight):
        small = fits(mesh, tokens, routes, router_weight, member_seeds, gate_weight)
        body = gathered if small else local
        return jax.shard_map(
            body, mesh=mesh, in_specs=in_specs, out_specs=out_specs, check_vma=False
        )(tokens, routes, router_weight, router_bias, member_seeds, gate_weight, up_weight)

    return whole
```

```python
import functools
import math

import jax
import jax.numpy as jnp
from jax import lax
from jax.experimental import pallas as pl
from jax.experimental.pallas import tpu as pltpu
from jax.sharding import PartitionSpec as P

FW = 1536
LENGTH = 512


NOISE = 0.25
ALPHA = 1.702


def noise_table(member_seeds, matrix_tag, expert, positions, expert_count):
    rank_index = jnp.arange(4, dtype=jnp.int32)
    counter = ((matrix_tag * expert_count + expert) * 4 + rank_index) * 4096
    counter = counter[None, None, :] + positions[:, None, None]
    hashed = (member_seeds[None, :, None] * 31 + counter) * 1103515245 + 12345
    hashed = hashed ^ hashed >> 16
    hashed = hashed * 747796405
    levels = (hashed >> 16 & 255) - 128
    return (levels.astype(jnp.float32) / 128.0).reshape(positions.shape[0], -1)


def expert_rows(
    inputs, transcripts, member_seeds, gate_cols, up_cols, expert, hidden_index, expert_count
):
    model_width = inputs.shape[1]
    members = member_seeds.shape[0]
    positions = jnp.arange(model_width, dtype=jnp.int32)
    left_factors = jnp.concatenate(
        [
            noise_table(member_seeds, 0, expert, positions, expert_count),
            noise_table(member_seeds, 1, expert, positions, expert_count),
        ],
        axis=1,
    ).astype(jnp.bfloat16)
    projected = jnp.dot(inputs, left_factors, preferred_element_type=jnp.float32)
    select = (transcripts[:, None] == jnp.arange(members, dtype=jnp.int32)[None, :]).astype(
        jnp.float32
    )
    select = jnp.repeat(select, 4, axis=1)
    noise_scale = NOISE / math.sqrt(model_width)
    gate_noise = jnp.dot(
        projected[:, : 4 * members] * select,
        noise_table(member_seeds, 2, expert, hidden_index, expert_count).T,
        precision=lax.Precision.HIGHEST,
    )
    up_noise = jnp.dot(
        projected[:, 4 * members :] * select,
        noise_table(member_seeds, 3, expert, hidden_index, expert_count).T,
        precision=lax.Precision.HIGHEST,
    )
    gate_sum = (
        jnp.dot(inputs, gate_cols, preferred_element_type=jnp.float32) + noise_scale * gate_noise
    )
    up_sum = jnp.dot(inputs, up_cols, preferred_element_type=jnp.float32) + noise_scale * up_noise
    return (gate_sum * jax.nn.sigmoid(ALPHA * gate_sum) * (up_sum + 1.0)).astype(jnp.bfloat16)


def local(tokens, routes, router_weight, router_bias, member_seeds, gate_weight, up_weight):
    tok_rows = tokens.shape[0]
    top_count = routes.shape[1]
    expert_count = router_weight.shape[1]
    quarter = gate_weight.shape[2]
    capacity = min(tok_rows, max(2, 2 * tok_rows * top_count // expert_count))
    device_count = lax.axis_size("exp")
    home_index = lax.axis_index("exp")
    core_index = lax.axis_index("tp")
    half_index = home_index % 2
    this_expert = home_index // 2
    partial_logits = jnp.dot(tokens, router_weight, preferred_element_type=jnp.float32)
    logits = lax.psum(partial_logits, "tp") + router_bias
    expert_ids = jnp.arange(expert_count, dtype=jnp.int32)
    chosen = jnp.sum(
        jnp.where(routes[:, :, None] == expert_ids[None, None, :], logits[:, None, :], 0.0), axis=2
    )
    weights = jax.nn.softmax(chosen, axis=1)
    flat_routes = routes.reshape(-1)
    entry_count = tok_rows * top_count
    flat_hot = (flat_routes[:, None] == expert_ids[None, :]).astype(jnp.int32)
    slot_index = jnp.sum((jnp.cumsum(flat_hot, axis=0) - 1) * flat_hot, axis=1)
    entry_rows = jnp.arange(entry_count, dtype=jnp.int32) // top_count
    entry_transcript = ((home_index * tok_rows + entry_rows) // LENGTH).astype(jnp.bfloat16)
    features = lax.all_gather(tokens, "tp", axis=1, tiled=True)
    feature_width = features.shape[1]
    entry_features = features[entry_rows]
    destination = jnp.concatenate([2 * flat_routes, 2 * flat_routes + 1])
    position = jnp.concatenate([slot_index, slot_index])
    payload = jnp.concatenate([entry_features, entry_features], axis=0)
    labels = jnp.concatenate([entry_transcript, entry_transcript])
    target = destination * capacity + position
    send_rows = (
        jnp.zeros((device_count * capacity, feature_width), jnp.bfloat16).at[target].set(payload)
    )
    send_rows = send_rows.reshape(device_count, capacity, feature_width)
    send_labels = jnp.full((device_count * capacity,), -1.0, jnp.bfloat16).at[target].set(labels)
    send_labels = send_labels.reshape(device_count, capacity)
    hidden_index = (
        half_index * (FW // 2) + core_index * quarter + jnp.arange(quarter, dtype=jnp.int32)
    )
    arrived_rows = lax.all_to_all(send_rows, "exp", split_axis=0, concat_axis=0, tiled=True)
    arrived_labels = lax.all_to_all(send_labels, "exp", split_axis=0, concat_axis=0, tiled=True)
    flat_rows = arrived_rows.reshape(-1, arrived_rows.shape[-1])
    transcripts = arrived_labels.reshape(-1).astype(jnp.int32)
    activation = expert_rows(
        flat_rows,
        transcripts,
        member_seeds,
        gate_weight[0],
        up_weight[0],
        this_expert,
        hidden_index,
        expert_count,
    )
    activation = activation.reshape(arrived_labels.shape + (quarter,))
    returned = lax.all_to_all(activation, "exp", split_axis=0, concat_axis=0, tiled=True)
    returned = returned.reshape(-1, quarter)
    pick_index = (
        (2 * flat_routes)[:, None] + jnp.arange(2, dtype=jnp.int32)[None, :]
    ) * capacity + slot_index[:, None]
    picked = returned[pick_index]
    routed = (picked.astype(jnp.float32) * weights.reshape(-1)[:, None, None]).astype(jnp.bfloat16)
    return routed.reshape(tok_rows, top_count, 2, quarter)


Z, X, C = 4, 2, 2
PIECES = 2
ROW = X * C
MESH = pl.DeviceIdType.MESH


def levels(seeds, counter):
    hashed = (seeds * 31 + counter) * 1103515245 + 12345
    hashed = hashed ^ (hashed >> 16)
    hashed = hashed * 747796405
    return (((hashed >> 16) & 255) - 128).astype(jnp.float32) / 128.0


def row_seeds(seed_ref, member, members):
    seeds = jnp.zeros_like(member)
    for index in range(members):
        seeds = jnp.where(member == index, seed_ref[index], seeds)
    return seeds


def fused(
    expert_count, seed_hbm, tokens, routes_hbm, router, bias_hbm, gate, up, out,
    seed_ref, routes, bias,
    held, wg, wu, gt, ut, left, act, back, gsend, grecv, rsend, rrecv, wsem,
):
    count = Z * ROW
    rows, width = held.shape[1:]
    hidden = wg.shape[1]
    members = seed_ref.shape[0]
    me = lax.axis_index("exp")
    z, x, c = me // ROW, (me // C) % X, me % C
    expert, half = me // 2, me % 2
    whole = width // 128 * 128
    rest = width - whole
    beside, sibling = me + C * (1 - 2 * x), me + 1 - 2 * c

    load = pltpu.make_async_copy(tokens, held.at[me], wsem.at[0])
    load.start()
    small = [
        pltpu.make_async_copy(source, target, wsem.at[3 + index])
        for index, (source, target) in enumerate(
            [(seed_hbm, seed_ref), (routes_hbm, routes), (bias_hbm, bias)]
        )
    ]
    for copy in small:
        copy.start()
    load_g = pltpu.make_async_copy(gate.at[0], wg, wsem.at[1])
    load_g.start()
    load_u = pltpu.make_async_copy(up.at[0], wu, wsem.at[2])
    load_u.start()

    barrier = pltpu.get_barrier_semaphore()

    def greet(k, carry):
        pl.semaphore_signal(
            barrier, inc=1, device_id={"exp": (me + k) % count}, device_id_type=MESH
        )
        return carry

    lax.fori_loop(1, count, greet, 0)
    load.wait()
    pl.semaphore_wait(barrier, count - 1)

    cut = rows // PIECES

    def pass_on(slot, piece, way, target):
        block = held.at[slot, pl.ds(piece * cut, cut)]
        return pltpu.make_async_remote_copy(
            src_ref=block, dst_ref=block,
            send_sem=gsend.at[slot, piece, way], recv_sem=grecv.at[slot, piece],
            device_id={"exp": target}, device_id_type=MESH,
        )

    def arrived(slot, piece):
        pass_on(slot, piece, 3, sibling).wait_recv()

    def give_back(slot):
        return pltpu.make_async_remote_copy(
            src_ref=act.at[slot], dst_ref=back.at[half, expert],
            send_sem=rsend.at[slot], recv_sem=rrecv.at[me],
            device_id={"exp": slot}, device_id_type=MESH,
        )

    for piece in range(PIECES):
        @pl.when(z < Z - 1)
        def _(piece=piece):
            pass_on(me, piece, 0, me + ROW).start()

        @pl.when(z > 0)
        def _(piece=piece):
            pass_on(me, piece, 1, me - ROW).start()

        pass_on(me, piece, 2, beside).start()
        pass_on(me, piece, 3, sibling).start()

    def chip_row(step):
        mirror = z // 2
        near = (z + mirror * (3 - 2 * z) + step) % Z
        return near + mirror * (3 - 2 * near)

    def relay(step, piece):
        above = step + 1

        @pl.when(z - above >= 0)
        def _():
            slot = me - above * ROW
            arrived(slot, piece)

            @pl.when(z < Z - 1)
            def _():
                pass_on(slot, piece, 0, me + ROW).start()

            @pl.when(z != 1)
            def _():
                pass_on(slot, piece, 2, beside).start()

            pass_on(slot, piece, 3, sibling).start()

        @pl.when(z + above < Z)
        def _():
            slot = me + above * ROW
            arrived(slot, piece)

            @pl.when(z > 0)
            def _():
                pass_on(slot, piece, 1, me - ROW).start()

            @pl.when(z != Z - 2)
            def _():
                pass_on(slot, piece, 2, beside).start()

            pass_on(slot, piece, 3, sibling).start()

        across = chip_row(step) * ROW + (1 - x) * C + c
        arrived(across, piece)
        pass_on(across, piece, 3, sibling).start()

        @pl.when((step == 0) & (z == 0))
        def _():
            pass_on(across, piece, 0, me + ROW).start()

        @pl.when((step == 0) & (z == Z - 1))
        def _():
            pass_on(across, piece, 1, me - ROW).start()

    for copy in small:
        copy.wait()
    noisy = 8 * members
    k = lax.broadcasted_iota(jnp.int32, (noisy, width), 0)
    i = lax.broadcasted_iota(jnp.int32, (noisy, width), 1)
    seeds = row_seeds(seed_ref, (k // 4) % members, members)
    number = ((k // (4 * members)) * expert_count + expert) * 4 + k % 4
    left[...] = levels(seeds, number * 4096 + i).astype(jnp.bfloat16)
    k = lax.broadcasted_iota(jnp.int32, (noisy, hidden), 0)
    i = lax.broadcasted_iota(jnp.int32, (noisy, hidden), 1) + half * hidden
    seeds = row_seeds(seed_ref, (k // 4) % members, members)
    number = ((2 + k // (4 * members)) * expert_count + expert) * 4 + k % 4
    right = levels(seeds, number * 4096 + i)
    for ref, tag in ((gt, 0), (ut, 1)):
        part = jnp.where(k // (4 * members) == tag, right, 0.0).astype(jnp.bfloat16)
        ref[rest:, :] = jnp.zeros((ref.shape[0] - rest, hidden), jnp.bfloat16)
        for piece in range(3):
            ref[rest + piece * noisy : rest + (piece + 1) * noisy, :] = part
    load_g.wait()
    load_u.wait()
    gt[0:rest, :] = wg[whole:, :]
    ut[0:rest, :] = wu[whole:, :]

    scale = NOISE / math.sqrt(width)
    batch = C * rows
    tile = 256

    def compute(base):
        values = held[pl.ds(base, C)].reshape(batch, width)
        projected = lax.dot_general(
            values, left[...], (((1,), (1,)), ((), ())), preferred_element_type=jnp.float32
        )
        where = base * rows + lax.broadcasted_iota(jnp.int32, (batch, noisy), 0)
        member = (lax.broadcasted_iota(jnp.int32, (batch, noisy), 1) // 4) % members
        remaining = jnp.where(where // LENGTH == member, projected * scale, 0.0)
        ends = [values[:, whole:]]
        for _ in range(3):
            piece = remaining.astype(jnp.bfloat16)
            remaining = remaining - piece.astype(jnp.float32)
            ends.append(piece)
        ends.append(jnp.zeros((batch, 128 - rest - 3 * noisy), jnp.bfloat16))
        end = jnp.concatenate(ends, axis=1)

        def columns(n, carry):
            at = pl.ds(pl.multiple_of(n * tile, tile), tile)
            start = held[pl.ds(base, C), :, 0:whole].reshape(batch, whole)
            g = jnp.dot(start, wg[0:whole, at], preferred_element_type=jnp.float32)
            g = g + jnp.dot(end, gt[:, at], preferred_element_type=jnp.float32)
            u = jnp.dot(start, wu[0:whole, at], preferred_element_type=jnp.float32)
            u = u + jnp.dot(end, ut[:, at], preferred_element_type=jnp.float32)
            value = (g * jax.nn.sigmoid(ALPHA * g) * (u + 1.0)).astype(jnp.bfloat16)
            act[pl.ds(base, C), :, at] = value.reshape(C, rows, tile)
            return carry

        lax.fori_loop(0, hidden // tile, columns, 0)

    def column(row):
        @pl.when((row >= 0) & (row < Z))
        def _():
            base = row * ROW + x * C
            for piece in range(PIECES):
                arrived(base + 1 - c, piece)
            compute(base)

            @pl.when(row // 2 != z // 2)
            def _():
                for other in range(C):
                    give_back(base + other).start()

    def far(step):
        for other in range(C):
            give_back(chip_row(step) * ROW + (1 - x) * C + other).start()

    middle = (z // 2 + z) % 2

    def visit(step, carry):
        def forward(piece, carry):
            relay(step, piece)
            return carry

        lax.fori_loop(0, PIECES, forward, 0)
        inward = 1 - 2 * (z // 2)
        column(z + inward * (step + 1))
        column(z - inward * (step + 1))
        base = chip_row(step) * ROW + (1 - x) * C
        for piece in range(PIECES):
            arrived(base + 1 - c, piece)
        compute(base)

        @pl.when(step == 2)
        def _():
            far(1)

            @pl.when(middle == 0)
            def _():
                far(2)

        return carry

    for piece in range(PIECES):
        arrived(sibling, piece)
    compute(me - c)
    lax.fori_loop(0, Z, visit, 0)
    @pl.when(middle == 0)
    def _():
        far(3)

    @pl.when(middle == 1)
    def _():
        far(2)
        far(3)

    near_row = z + 1 - 2 * (z % 2)
    for other in range(C):
        give_back(near_row * ROW + x * C + other).start()
    give_back(beside).start()
    give_back(beside + 1 - 2 * c).start()
    give_back(sibling).start()
    back[half, expert] = act[me]

    top = routes.shape[0]
    logits = lax.dot_general(
        held[me], router[...], (((1,), (1,)), ((), ())), preferred_element_type=jnp.float32
    )
    logits = logits + bias[...]
    ids = lax.broadcasted_iota(jnp.int32, logits.shape, 1).astype(jnp.float32)
    line = lax.broadcasted_iota(jnp.int32, (rows, rows), 0)
    unit = jnp.where(line == lax.broadcasted_iota(jnp.int32, (rows, rows), 1), 1.0, 0.0)
    named = lax.dot_general(
        unit.astype(jnp.bfloat16), routes[...].astype(jnp.float32).astype(jnp.bfloat16),
        (((1,), (1,)), ((), ())), preferred_element_type=jnp.float32,
    )
    chosen = [
        jnp.sum(jnp.where(named[:, j : j + 1] == ids, logits, 0.0), axis=1, keepdims=True)
        for j in range(top)
    ]
    peak = functools.reduce(jnp.maximum, chosen)
    grown = [jnp.exp(v - peak) for v in chosen]
    total = sum(grown[1:], grown[0])
    lines = rows * top * 2
    line = lax.broadcasted_iota(jnp.int32, (lines, rows), 0)
    spread = jnp.where(
        line // (2 * top) == lax.broadcasted_iota(jnp.int32, (lines, rows), 1), 1.0, 0.0
    ).astype(jnp.bfloat16)
    line = lax.broadcasted_iota(jnp.int32, (lines, 1), 0)
    weights = jnp.zeros((lines, 1), jnp.float32)
    choice = jnp.zeros((lines, 1), jnp.float32)
    for j in range(top):
        rest_j = grown[j] / total
        columns_j = [named[:, j : j + 1].astype(jnp.bfloat16)]
        for _ in range(3):
            piece = rest_j.astype(jnp.bfloat16)
            rest_j = rest_j - piece.astype(jnp.float32)
            columns_j.append(piece)
        wide = jnp.dot(
            spread, jnp.concatenate(columns_j, axis=1), preferred_element_type=jnp.float32
        )
        mine = (line // 2) % top == j
        choice = jnp.where(mine, wide[:, 0:1], choice)
        weights = jnp.where(mine, wide[:, 1:2] + wide[:, 2:3] + wide[:, 3:4], weights)
    source = (line % 2) * (expert_count * rows) + line // (2 * top)
    source = source + choice.astype(jnp.int32) * rows
    place = lax.broadcasted_iota(jnp.int32, (lines, 2 * expert_count * rows), 1)
    pick = jnp.where(place == source, 1.0, 0.0).astype(jnp.bfloat16)

    def take(k, carry):
        slot = (me + k) % count
        pltpu.make_async_remote_copy(
            src_ref=act.at[slot], dst_ref=back.at[slot % 2, slot // 2],
            send_sem=rsend.at[slot], recv_sem=rrecv.at[slot],
            device_id={"exp": slot}, device_id_type=MESH,
        ).wait_recv()
        return carry

    lax.fori_loop(1, count, take, 0)
    found = jnp.dot(
        pick, back[...].reshape(2 * expert_count * rows, hidden), preferred_element_type=jnp.float32
    )
    out[...] = (found * weights).astype(jnp.bfloat16).reshape(rows * top, 2, hidden)

    def sent(k, carry):
        slot = (me + k) % count
        give_back(slot).wait_send()
        return carry

    lax.fori_loop(1, count, sent, 0)

    def passed(k, carry):
        zo, piece = k // PIECES, k % PIECES
        slot = zo * ROW + x * C + c

        @pl.when((zo <= z) & (z < Z - 1))
        def _():
            pass_on(slot, piece, 0, me + ROW).wait_send()

        @pl.when((zo >= z) & (z > 0))
        def _():
            pass_on(slot, piece, 1, me - ROW).wait_send()

        @pl.when(((z != 1) | (zo != 0)) & ((z != Z - 2) | (zo != Z - 1)))
        def _():
            pass_on(slot, piece, 2, beside).wait_send()

        @pl.when((zo == 0) & (z == 0))
        def _():
            pass_on(zo * ROW + (1 - x) * C + c, piece, 0, me + ROW).wait_send()

        @pl.when((zo == Z - 1) & (z == Z - 1))
        def _():
            pass_on(zo * ROW + (1 - x) * C + c, piece, 1, me - ROW).wait_send()

        pass_on(slot, piece, 3, sibling).wait_send()
        pass_on(zo * ROW + (1 - x) * C + c, piece, 3, sibling).wait_send()
        return carry

    lax.fori_loop(0, PIECES * Z, passed, 0)


def gathered(tokens, routes, router_weight, router_bias, member_seeds, gate_weight, up_weight):
    rows, width = tokens.shape
    top = routes.shape[1]
    expert_count = router_weight.shape[1]
    hidden = gate_weight.shape[2]
    count = Z * ROW
    noisy = 8 * member_seeds.shape[0]
    vmem = pl.BlockSpec(memory_space=pltpu.VMEM)
    anywhere = pl.BlockSpec(memory_space=pl.ANY)
    half_dtype = jnp.bfloat16
    result = pl.pallas_call(
        functools.partial(fused, expert_count),
        out_shape=jax.ShapeDtypeStruct((top * rows, 2, hidden), half_dtype),
        in_specs=[anywhere] * 3 + [vmem] + [anywhere] * 3,
        out_specs=vmem,
        scratch_shapes=[
            pltpu.SMEM(member_seeds.shape, jnp.int32),
            pltpu.VMEM((top, rows), jnp.int32),
            pltpu.VMEM((1, expert_count), jnp.float32),
            pltpu.VMEM((count, rows, width), half_dtype),
            pltpu.VMEM((width, hidden), half_dtype),
            pltpu.VMEM((width, hidden), half_dtype),
            pltpu.VMEM((128, hidden), half_dtype),
            pltpu.VMEM((128, hidden), half_dtype),
            pltpu.VMEM((noisy, width), half_dtype),
            pltpu.VMEM((count, rows, hidden), half_dtype),
            pltpu.VMEM((2, expert_count, rows, hidden), half_dtype),
            pltpu.SemaphoreType.DMA((count, PIECES, 4)),
            pltpu.SemaphoreType.DMA((count, PIECES)),
            pltpu.SemaphoreType.DMA((count,)),
            pltpu.SemaphoreType.DMA((count,)),
            pltpu.SemaphoreType.DMA((6,)),
        ],
        compiler_params=pltpu.CompilerParams(
            collective_id=0, has_side_effects=True, vmem_limit_bytes=60 * 1024 * 1024
        ),
        cost_estimate=pl.CostEstimate(
            flops=4 * count * rows * width * hidden,
            bytes_accessed=4 * width * hidden,
            transcendentals=count * rows * hidden,
        ),
    )(
        member_seeds, tokens, routes.T, router_weight.T, router_bias[None, :], gate_weight, up_weight
    )
    return result.reshape(rows, top, 2, hidden)


def fits(mesh, tokens, routes, router_weight, member_seeds, gate_weight):
    devices = mesh.shape["exp"]
    rows = tokens.shape[0] // (mesh.shape["pop"] * devices)
    experts = router_weight.shape[1]
    return (
        mesh.shape["tp"] == 1
        and devices == Z * ROW == 2 * experts
        and 2 * rows * routes.shape[1] // experts >= rows
        and tokens.shape[1] % 128 + 24 * (member_seeds.shape[0] // mesh.shape["pop"]) <= 128
        and gate_weight.shape[2] % 256 == 0
    )


def solution(mesh):
    in_specs = (
        P(("pop", "exp"), "tp"),
        P(("pop", "exp"), None),
        P("tp", None),
        P(),
        P("pop"),
        P("exp", None, "tp"),
        P("exp", None, "tp"),
    )
    out_specs = P(("pop", "exp"), None, None, "tp")

    def whole(tokens, routes, router_weight, router_bias, member_seeds, gate_weight, up_weight):
        small = fits(mesh, tokens, routes, router_weight, member_seeds, gate_weight)
        body = gathered if small else local
        return jax.shard_map(
            body, mesh=mesh, in_specs=in_specs, out_specs=out_specs, check_vma=False
        )(tokens, routes, router_weight, router_bias, member_seeds, gate_weight, up_weight)

    return whole
```
